768 devices in a mesh: dpx: 8 (over y_hi, x), dpy: 96 (over y_lo, z, core).
Axes of the slice: x: 4, y: 8 (y_hi: 2, y_lo: 4; y = y_hi * 4 + y_lo), z: 12, core: 2. Of those that a mesh axis runs over, the one named last changes fastest.
Arguments:
- tokens: bfloat16 [294912, 4608], P(('dpx', 'dpy')), may hold values from -24 to 24
- cotangents: bfloat16 [2, 294912, 128], P(None, ('dpx', 'dpy')), may hold values from -0.02734375 to 0.02734375
- params: float32 [2, 4608, 128], P(None, ('dpx', 'dpy')), may hold values from -0.75 to 0.75
- moment: float32 [2, 4608, 128], P(None, ('dpx', 'dpy')), may hold values from -4 to 4
- second: float32 [2, 4608, 128], P(None, ('dpx', 'dpy')), may hold values from 0.01 to 1
Outputs:
- new_params: float32 [2, 4608, 128], P(None, ('dpx', 'dpy'))
- new_moment: float32 [2, 4608, 128], P(None, ('dpx', 'dpy'))
- new_second: float32 [2, 4608, 128], P(None, ('dpx', 'dpy'))
- gathered: bfloat16 [2, 4608, 128], replicated
The draws below stay inside these ranges and needn't reach their ends.
All inputs are finite; a program needn't handle non-finite values.
Results may differ from the reference program's by a relative error of at most 0.0059.
Values may be sent and summed in bfloat16 or wider, within the bound.
No kernel may reach another device: no remote copies, remote signals or barrier semaphores. Data moves between devices by JAX's collectives and lax.ppermute only.
A program may use at most 32 MiB of HBM per device.

```python
import math
import jax
import jax.numpy as jnp
from jax import lax

D = 4608
COLS = 128
BUCKETS = 2
TOKENS = 294912


def with_spikes(result, own_key, source, target, shards_of, factor):
    def block_of(axis_at):
        return (jnp.arange(result.shape[axis_at]) // (result.shape[axis_at] // shards_of)).reshape((-1,) + (1,) * (result.ndim - 1 - axis_at))

    one_side = jax.random.permutation(own_key, shards_of)[block_of(target)]
    other_side = (block_of(target) + shards_of // 2) % shards_of
    return jnp.where((block_of(source) == one_side) | (block_of(source) == other_side), factor * result, result)


def levels(rng, dims, pieces, low, top_value):
    level, own = 1.0, jax.random.fold_in(rng, 6)
    for position, shards_of in pieces:
        draws = jnp.exp(jax.random.uniform(jax.random.fold_in(own, position), (shards_of,), jnp.float32, low / len(pieces), top_value / len(pieces)))
        level = level * jnp.repeat(draws, dims[position] // shards_of).reshape([-1 if axis == position else 1 for axis in range(len(dims))])
    return level


def bell_draw(own_key, extent, deviation, reach, pieces=(), dtype=jnp.bfloat16):
    gain = levels(own_key, extent, pieces, -0.22, 0.18) if pieces else 1.0
    drawn = jax.random.normal(own_key, extent, jnp.float32) * deviation * gain
    return jnp.minimum(jnp.maximum(drawn, -reach), reach).astype(dtype)


def heavy_noise(rng, shape, spread, reach, split, heavy, held_as=jnp.bfloat16):
    array = spread * jax.random.normal(rng, shape, jnp.float32)
    if split:
        array = array * levels(rng, shape, split, -0.22, 0.18)
    return jnp.clip(with_spikes(array, jax.random.fold_in(rng, 3), *heavy), -reach, reach).astype(held_as)


def setup_inputs(seed: int = 0) -> dict:
    splits = jax.random.split(jax.random.key(seed), 6)
    return {
        "tokens": heavy_noise(splits[0], (TOKENS, D), 1.0, 24.0, ((0, 768),), (0, 1, 768, 6.0)),
        "cotangents": bell_draw(splits[1], (BUCKETS, TOKENS, COLS), (TOKENS ** -0.5), 0.02734375, ((1, 768),)),
        "params": bell_draw(splits[2], (BUCKETS, D, COLS), 0.05, 0.75, ((1, 768),), jnp.float32),
        "moment": bell_draw(splits[3], (BUCKETS, D, COLS), 0.3, 4.0, ((1, 768),), jnp.float32),
        "second": jnp.clip(jnp.exp(math.log(1.0) - 4.6051702 * jax.random.uniform(splits[4], (BUCKETS, D, COLS), jnp.float32) ** levels(splits[4], (BUCKETS, D, COLS), ((1, 768),), -0.2, 0.2)), 0.01, 1.0),
    }


def reference(tokens, cotangents, params, moment, second):

    def one_bucket(cotangent):
        return lax.dot_general(tokens, cotangent, (((0,), (0,)), ((), ())), preferred_element_type=jnp.float32)
    gradient = lax.map(one_bucket, cotangents)
    new_moment = 0.9 * moment + 0.1 * gradient
    new_second = 0.95 * second + 0.05 * gradient * gradient
    first_fix = 1.0 - 0.9 ** 10
    second_fix = 1.0 - 0.95 ** 10
    update = new_moment / first_fix / (jnp.sqrt(new_second / second_fix) + 1e-08)
    new_params = params - 0.01 * (update + 0.1 * params)
    return (new_params, new_moment, new_second, new_params.astype(jnp.bfloat16))
```

```python
import jax
import jax.numpy as jnp
from jax import lax
from jax.sharding import Mesh
from jax.sharding import PartitionSpec as P

ALL = ("yh", "x", "yl", "yp", "z", "core")
SIZES = (2, 4, 2, 2, 12, 2)
NEAR = ("x", "yp")
FAR = ("yh", "yl", "z")
SWAP = [(0, 1), (1, 0)]


def exchange(blocks, axes):
    return lax.all_to_all(blocks, axes, 0, 0, tiled=True)


def total(blocks):
    return blocks.astype(jnp.float32).sum(0)


def adam(gradient, params, moment, second):
    new_moment = 0.9 * moment + 0.1 * gradient
    new_second = 0.95 * second + 0.05 * gradient * gradient
    first_fix = 1.0 - 0.9**10
    second_fix = 1.0 - 0.95**10
    update = new_moment / first_fix / (jnp.sqrt(new_second / second_fix) + 1e-08)
    new_params = params - 0.01 * (update + 0.1 * params)
    return new_params, new_moment, new_second


def on_device(tokens, cotangents, params, moment, second):
    core = lax.axis_index("core")

    def local_gradient(bucket):
        cotangent = lax.dynamic_index_in_dim(cotangents, bucket, 0, False)
        return lax.dot_general(
            tokens, cotangent, (((0,), (0,)), ((), ())), preferred_element_type=jnp.float32
        ).astype(jnp.bfloat16)

    away = lax.ppermute(local_gradient(1 - core), "core", SWAP)
    state = jnp.stack([params, moment, second])
    away_state = lax.dynamic_index_in_dim(state, 1 - core, 1, False)
    home_state = lax.dynamic_index_in_dim(state, core, 1, False)
    other_state = lax.ppermute(away_state, "core", SWAP)
    home = lax.optimization_barrier(local_gradient(core))
    part = (home.astype(jnp.float32) + away.astype(jnp.float32)).astype(jnp.bfloat16)

    near = part.reshape(2, 4, 2, 2, 144, 128).transpose(1, 3, 0, 2, 4, 5).reshape(8, 576, 128)
    near = total(exchange(near, NEAR)).astype(jnp.bfloat16)
    gradient = total(exchange(near.reshape(48, 12, 128), FAR))

    first = core == 0
    rows_state = jnp.where(
        first,
        jnp.concatenate([home_state, other_state], axis=1),
        jnp.concatenate([other_state, home_state], axis=1),
    )
    rounded = adam(gradient, *rows_state)[0].astype(jnp.bfloat16)

    keep = jnp.where(first, gradient[:6], gradient[6:])
    other = lax.ppermute(jnp.where(first, gradient[6:], gradient[:6]), "core", SWAP)
    both = jnp.where(first, jnp.stack([keep, other]), jnp.stack([other, keep]))
    new_params, new_moment, new_second = adam(both, params, moment, second)

    far = exchange(jnp.broadcast_to(rounded, (48, 12, 128)), FAR).reshape(576, 128)
    near = exchange(jnp.broadcast_to(far, (8, 576, 128)), NEAR)
    mine = near.reshape(4, 2, 2, 2, 144, 128).transpose(2, 0, 3, 1, 4, 5).reshape(4608, 128)
    theirs = lax.ppermute(mine, "core", SWAP)
    gathered = jnp.where(first, jnp.stack([mine, theirs]), jnp.stack([theirs, mine]))
    return (new_params, new_moment, new_second, gathered)


def solution(mesh):
    fine = Mesh(mesh.devices.reshape(SIZES), ALL)
    rows = P(None, ALL, None)
    return jax.shard_map(
        on_device,
        mesh=fine,
        in_specs=(P(ALL, None), rows, rows, rows, rows),
        out_specs=(rows, rows, rows, P()),
        check_vma=False,
    )
```

```python
import functools

import jax
import jax.numpy as jnp
import numpy as np
from jax import lax
from jax.experimental import pallas as pl
from jax.experimental.pallas import tpu as pltpu
from jax.sharding import Mesh
from jax.sharding import PartitionSpec as P

ALL = ("yh", "x", "yl", "yp", "zl", "zp", "core")
SIZES = (2, 4, 2, 2, 6, 2, 2)
NEAR = ("x", "yp", "zp")
FAR = ("yh", "yl", "zl")
N_NEAR, N_FAR = 16, 24
SWAP = [(0, 1), (1, 0)]
ROWS = 6
HALF = 2304
CHUNK = 768
COLS = 128

_at = np.indices(SIZES).reshape(len(SIZES), -1)
_at = dict(zip(ALL, _at))
HOLDS = (
    _at["core"] * (N_NEAR * N_FAR)
    + ((_at["x"] * 2 + _at["yp"]) * 2 + _at["zp"]) * N_FAR
    + (_at["yh"] * 2 + _at["yl"]) * 6
    + _at["zl"]
)
TO_OWNER = [(holder, int(owner)) for holder, owner in enumerate(HOLDS)]
TO_HOLDER = [(owner, holder) for holder, owner in TO_OWNER]

VMEM = pl.BlockSpec(memory_space=pltpu.VMEM)


def exchange(blocks, axes):
    return lax.all_to_all(blocks, axes, 0, 0, tiled=True)


def total(blocks):
    return blocks.astype(jnp.float32).sum(0)


def gradient_kernel(other, tokens, cotangents, out, held, arrived):
    core = lax.axis_index("core")
    half = 1 - core if other else core
    copies = []
    for step in range(HALF // CHUNK):
        first = pl.multiple_of(half * HALF + step * CHUNK, COLS)
        copies.append(
            pltpu.make_async_copy(
                tokens.at[:, pl.ds(first, CHUNK)], held.at[step], arrived.at[step]
            )
        )
        copies[-1].start()
    both = jnp.concatenate([cotangents[0], cotangents[1]], axis=1)
    for step, copy in enumerate(copies):
        copy.wait()
        out[step * CHUNK : (step + 1) * CHUNK, :] = lax.dot_general(
            held[step], both, (((0,), (0,)), ((), ())), preferred_element_type=jnp.float32
        ).astype(out.dtype)


def local_gradient(tokens, cotangents, other):
    count = tokens.shape[0]
    return pl.pallas_call(
        functools.partial(gradient_kernel, other),
        out_shape=jax.ShapeDtypeStruct((HALF, 2 * COLS), jnp.bfloat16),
        in_specs=[pl.BlockSpec(memory_space=pltpu.HBM), VMEM],
        out_specs=VMEM,
        scratch_shapes=[
            pltpu.VMEM((HALF // CHUNK, count, CHUNK), jnp.bfloat16),
            pltpu.SemaphoreType.DMA((HALF // CHUNK,)),
        ],
        compiler_params=pltpu.CompilerParams(vmem_limit_bytes=60_000_000),
        cost_estimate=pl.CostEstimate(
            flops=2 * count * HALF * 2 * COLS, bytes_accessed=count * HALF * 2, transcendentals=0
        ),
        name="gradient_kernel",
    )(tokens, cotangents)


def sum_kernel(blocks, out, held):
    held[...] = blocks[...].astype(jnp.float32).sum(0)
    for index in range(N_FAR):
        out[index] = held[index * ROWS : (index + 1) * ROWS, :].astype(out.dtype)


def sum_near(blocks):
    return pl.pallas_call(
        sum_kernel,
        out_shape=jax.ShapeDtypeStruct((N_FAR, ROWS, 2 * COLS), jnp.bfloat16),
        in_specs=[VMEM],
        out_specs=VMEM,
        scratch_shapes=[pltpu.VMEM((N_FAR * ROWS, 2 * COLS), jnp.float32)],
        compiler_params=pltpu.CompilerParams(vmem_limit_bytes=24 * 2**20),
        name="sum_kernel",
    )(blocks)


def spread_kernel(blocks, out, held):
    for index in range(N_FAR):
        held[index * ROWS : (index + 1) * ROWS, :] = blocks[index].astype(jnp.float32)
    rows = held[...].astype(out.dtype)
    for index in range(N_NEAR):
        out[index] = rows


def spread_far(blocks):
    return pl.pallas_call(
        spread_kernel,
        out_shape=jax.ShapeDtypeStruct((N_NEAR, N_FAR * ROWS, 2 * COLS), jnp.bfloat16),
        in_specs=[VMEM],
        out_specs=VMEM,
        scratch_shapes=[pltpu.VMEM((N_FAR * ROWS, 2 * COLS), jnp.float32)],
        compiler_params=pltpu.CompilerParams(vmem_limit_bytes=24 * 2**20),
        name="spread_kernel",
    )(blocks)


def adam(gradient, params, moment, second):
    new_moment = 0.9 * moment + 0.1 * gradient
    new_second = 0.95 * second + 0.05 * gradient * gradient
    first_fix = 1.0 - 0.9**10
    second_fix = 1.0 - 0.95**10
    update = new_moment / first_fix / (jnp.sqrt(new_second / second_fix) + 1e-08)
    new_params = params - 0.01 * (update + 0.1 * params)
    return new_params, new_moment, new_second


def on_device(tokens, cotangents, params, moment, second):
    first = lax.axis_index("core") == 0

    away = lax.ppermute(local_gradient(tokens, cotangents, True), "core", SWAP)
    home = local_gradient(tokens, cotangents, False)
    part = (home.astype(jnp.float32) + away.astype(jnp.float32)).astype(jnp.bfloat16)

    state = jnp.stack([jnp.concatenate([a[0], a[1]], axis=1) for a in (params, moment, second)])
    state, part = lax.optimization_barrier((state, part))
    held = lax.ppermute(state, ALL, TO_HOLDER)

    near = exchange(part.reshape(N_NEAR, N_FAR * ROWS, 2 * COLS), NEAR)
    gradient = total(exchange(sum_near(near), FAR))
    rounded = adam(gradient, *held)[0].astype(jnp.bfloat16)

    far = exchange(jnp.broadcast_to(rounded, (N_FAR, ROWS, 2 * COLS)), FAR)

    owned = lax.ppermute(gradient, ALL, TO_OWNER)
    owned = jnp.stack([owned[:, :COLS], owned[:, COLS:]])
    new_params, new_moment, new_second = adam(owned, params, moment, second)

    mine = exchange(spread_far(far), NEAR).reshape(HALF, 2 * COLS)
    theirs = lax.ppermute(mine, "core", SWAP)
    rows = jnp.concatenate([jnp.where(first, mine, theirs), jnp.where(first, theirs, mine)])
    gathered = jnp.stack([rows[:, :COLS], rows[:, COLS:]])
    return (new_params, new_moment, new_second, gathered)


def solution(mesh):
    fine = Mesh(mesh.devices.reshape(SIZES), ALL)
    rows = P(None, ALL, None)
    return jax.shard_map(
        on_device,
        mesh=fine,
        in_specs=(P(ALL, None), rows, rows, rows, rows),
        out_specs=(rows, rows, rows, P()),
        check_vma=False,
    )
```

```python
import functools

import jax
import jax.numpy as jnp
from jax import lax
from jax.experimental import pallas as pl
from jax.experimental.pallas import tpu as pltpu
from jax.sharding import Mesh
from jax.sharding import PartitionSpec as P

ALL = ("yh", "x", "yl", "yp", "z", "core")
SIZES = (2, 4, 2, 2, 12, 2)
NEAR = ("x", "yp")
FAR = ("yh", "yl", "z")
SWAP = [(0, 1), (1, 0)]
N_NEAR, N_FAR = 8, 48
D, COLS = 4608, 128
ROWS = 12
BLOCK = 144
STEP = 1152

VMEM = pl.BlockSpec(memory_space=pltpu.VMEM)
PARAMS = pltpu.CompilerParams(vmem_limit_bytes=24 * 2**20)
NEAR_BLOCKS = jax.ShapeDtypeStruct((N_NEAR, N_FAR * ROWS, COLS), jnp.bfloat16)


def exchange(blocks, axes):
    return lax.all_to_all(blocks, axes, 0, 0, tiled=True)


def place(block):
    yh, x, yl, yp = block // 16, block // 4 % 4, block // 2 % 2, block % 2
    return x * 2 + yp, (yh * 2 + yl) * BLOCK


def gradient_kernel(other, tokens, cotangents, out):
    core = lax.axis_index("core")
    bucket = 1 - core if other else core
    turned = cotangents[bucket].astype(jnp.float32).T.astype(jnp.bfloat16)
    for step in range(D // STEP):
        product = jnp.dot(
            turned, tokens[:, step * STEP : (step + 1) * STEP], preferred_element_type=jnp.float32
        )
        rows = product.astype(out.dtype).T
        for part in range(STEP // BLOCK):
            chip, first = place(step * (STEP // BLOCK) + part)
            out[chip, first : first + BLOCK, :] = rows[part * BLOCK : (part + 1) * BLOCK, :]


def local_gradient(tokens, cotangents, other):
    count = tokens.shape[0]
    return pl.pallas_call(
        functools.partial(gradient_kernel, other),
        out_shape=NEAR_BLOCKS,
        in_specs=[VMEM, VMEM],
        out_specs=VMEM,
        compiler_params=PARAMS,
        cost_estimate=pl.CostEstimate(
            flops=2 * count * D * COLS, bytes_accessed=count * D * 2, transcendentals=0
        ),
        name="gradient_kernel",
    )(tokens, cotangents)


def add_kernel(left, right, out):
    out[...] = (left[...].astype(jnp.float32) + right[...].astype(jnp.float32)).astype(out.dtype)


def add(left, right):
    return pl.pallas_call(
        add_kernel,
        out_shape=NEAR_BLOCKS,
        in_specs=[VMEM, VMEM],
        out_specs=VMEM,
        compiler_params=PARAMS,
        name="add_kernel",
    )(left, right)


def sum_kernel(blocks, out, held):
    held[...] = blocks[...].astype(jnp.float32).sum(0)
    for index in range(N_FAR):
        out[index] = held[index * ROWS : (index + 1) * ROWS, :].astype(out.dtype)


def sum_near(blocks):
    return pl.pallas_call(
        sum_kernel,
        out_shape=jax.ShapeDtypeStruct((N_FAR, ROWS, COLS), jnp.bfloat16),
        in_specs=[VMEM],
        out_specs=VMEM,
        scratch_shapes=[pltpu.VMEM((N_FAR * ROWS, COLS), jnp.float32)],
        compiler_params=PARAMS,
        name="sum_kernel",
    )(blocks)


def spread_kernel(blocks, out, held):
    for index in range(N_FAR):
        held[index * ROWS : (index + 1) * ROWS, :] = blocks[index].astype(jnp.float32)
    rows = held[...].astype(out.dtype)
    for index in range(N_NEAR):
        out[index] = rows


def spread_far(blocks):
    return pl.pallas_call(
        spread_kernel,
        out_shape=NEAR_BLOCKS,
        in_specs=[VMEM],
        out_specs=VMEM,
        scratch_shapes=[pltpu.VMEM((N_FAR * ROWS, COLS), jnp.float32)],
        compiler_params=PARAMS,
        name="spread_kernel",
    )(blocks)


def write_kernel(other, *refs):
    blocks, out, done = refs[0], refs[-2], refs[-1]
    core = lax.axis_index("core")
    bucket = 1 - core if other else core
    copies = []
    for x in range(4):
        for yp in range(2):
            copies.append(
                pltpu.make_async_copy(
                    blocks.at[x, yp], out.at[bucket, :, x, :, yp], done.at[x * 2 + yp]
                )
            )
            copies[-1].start()
    for copy in copies:
        copy.wait()


def write_bucket(blocks, other, out=None):
    shape = (2, 2, 4, 2, 2, BLOCK, COLS)
    whole = pl.BlockSpec(memory_space=pl.ANY)
    blocks = blocks.reshape(4, 2, 2, 2, BLOCK, COLS)
    return pl.pallas_call(
        functools.partial(write_kernel, other),
        out_shape=jax.ShapeDtypeStruct(shape, jnp.bfloat16),
        in_specs=[VMEM] if out is None else [VMEM, whole],
        out_specs=whole,
        scratch_shapes=[pltpu.SemaphoreType.DMA((N_NEAR,))],
        input_output_aliases={} if out is None else {1: 0},
        compiler_params=PARAMS,
        cost_estimate=pl.CostEstimate(flops=0, bytes_accessed=2 * D * COLS * 2, transcendentals=0),
        name="write_kernel",
    )(*([blocks] if out is None else [blocks, out]))


def adam(gradient, params, moment, second):
    new_moment = 0.9 * moment + 0.1 * gradient
    new_second = 0.95 * second + 0.05 * gradient * gradient
    first_fix = 1.0 - 0.9**10
    second_fix = 1.0 - 0.95**10
    update = new_moment / first_fix / (jnp.sqrt(new_second / second_fix) + 1e-08)
    new_params = params - 0.01 * (update + 0.1 * params)
    return new_params, new_moment, new_second


def in_order(first, home, other, axis):
    return jnp.concatenate([jnp.where(first, home, other), jnp.where(first, other, home)], axis=axis)


def on_device(tokens, cotangents, params, moment, second):
    first = lax.axis_index("core") == 0

    away = lax.ppermute(local_gradient(tokens, cotangents, True), "core", SWAP)
    part = add(local_gradient(tokens, cotangents, False), away)

    state = jnp.stack([params, moment, second], axis=1)
    state, part = lax.optimization_barrier((state, part))
    home_state = jnp.where(first, state[0], state[1])
    other_state = lax.ppermute(jnp.where(first, state[1], state[0]), "core", SWAP)
    held = in_order(first, home_state, other_state, 1)

    near = sum_near(exchange(part, NEAR))
    near, held = lax.optimization_barrier((near, held))
    gradient = exchange(near, FAR).astype(jnp.float32).sum(0)
    rounded = adam(gradient, *held)[0].astype(jnp.bfloat16)
    far = exchange(jnp.broadcast_to(rounded, (N_FAR, ROWS, COLS)), FAR)

    keep = jnp.where(first, gradient[:6], gradient[6:])
    other = lax.ppermute(jnp.where(first, gradient[6:], gradient[:6]), "core", SWAP)
    owned = in_order(first, keep[None], other[None], 0)
    new_params, new_moment, new_second = adam(owned, params, moment, second)
    far, new_params, new_moment, new_second = lax.optimization_barrier(
        (far, new_params, new_moment, new_second)
    )

    mine = exchange(spread_far(far), NEAR)
    theirs = lax.ppermute(mine, "core", SWAP)
    gathered = write_bucket(theirs, True, write_bucket(mine, False))
    return (new_params, new_moment, new_second, gathered.reshape(2, D, COLS))


def solution(mesh):
    fine = Mesh(mesh.devices.reshape(SIZES), ALL)
    rows = P(None, ALL, None)
    return jax.shard_map(
        on_device,
        mesh=fine,
        in_specs=(P(ALL, None), rows, rows, rows, rows),
        out_specs=(rows, rows, rows, P()),
        check_vma=False,
    )
```

```python
import functools

import jax
import jax.numpy as jnp
from jax import lax
from jax.experimental import pallas as pl
from jax.experimental.pallas import tpu as pltpu
from jax.sharding import Mesh
from jax.sharding import PartitionSpec as P

ALL = ("yh", "x", "yl", "yp", "z", "core")
SIZES = (2, 4, 2, 2, 12, 2)
NEAR = ("x", "yp")
FAR = ("yh", "yl", "z")
SWAP = [(0, 1), (1, 0)]
N_NEAR, N_FAR = 8, 48
D, COLS = 4608, 128
ROWS = 12
BLOCK = 144
STEP = 1152

VMEM = pl.BlockSpec(memory_space=pltpu.VMEM)
PARAMS = pltpu.CompilerParams(vmem_limit_bytes=24 * 2**20)
NEAR_BLOCKS = pltpu.VMEM((N_NEAR, N_FAR * ROWS, COLS), jnp.bfloat16)
FAR_BLOCKS = pltpu.VMEM((N_FAR, ROWS, COLS), jnp.bfloat16)


def exchange(blocks, axes):
    return lax.all_to_all(blocks, axes, 0, 0, tiled=True)


def place(block):
    yh, x, yl, yp = block // 16, block // 4 % 4, block // 2 % 2, block % 2
    return x * 2 + yp, (yh * 2 + yl) * BLOCK


def multiply(tokens, cotangent, out, columns):
    turned = cotangent.astype(jnp.float32).T.astype(jnp.bfloat16)
    for step in columns:
        product = jnp.dot(
            turned, tokens[:, step * STEP : (step + 1) * STEP], preferred_element_type=jnp.float32
        )
        rows = product.astype(out.dtype).T
        for part in range(STEP // BLOCK):
            chip, first = place(step * (STEP // BLOCK) + part)
            out[chip, first : first + BLOCK, :] = rows[part * BLOCK : (part + 1) * BLOCK, :]


def first_kernel(tokens, cotangents, out, held, small, arrived):
    other = 1 - lax.axis_index("core")
    copies = [pltpu.make_async_copy(cotangents, small, arrived.at[2])]
    for half in range(2):
        columns = (slice(None), pl.ds(half * (D // 2), D // 2))
        copies.append(
            pltpu.make_async_copy(tokens.at[columns], held.at[columns], arrived.at[half])
        )
    for copy in copies:
        copy.start()
    copies[0].wait()
    for half in range(2):
        copies[1 + half].wait()
        multiply(held, small[other], out, (2 * half, 2 * half + 1))


def second_kernel(tokens, cotangents, out):
    multiply(tokens, cotangents[lax.axis_index("core")], out, range(D // STEP))


def first_gradient(tokens, cotangents):
    return pl.pallas_call(
        first_kernel,
        out_shape=[
            NEAR_BLOCKS,
            pltpu.VMEM(tokens.shape, jnp.bfloat16),
            pltpu.VMEM(cotangents.shape, jnp.bfloat16),
        ],
        in_specs=[pl.BlockSpec(memory_space=pltpu.HBM)] * 2,
        out_specs=[VMEM] * 3,
        scratch_shapes=[pltpu.SemaphoreType.DMA((3,))],
        compiler_params=pltpu.CompilerParams(vmem_limit_bytes=55_000_000),
        name="first_kernel",
    )(tokens, cotangents)


def second_gradient(tokens, cotangents):
    return pl.pallas_call(
        second_kernel,
        out_shape=NEAR_BLOCKS,
        in_specs=[VMEM, VMEM],
        out_specs=VMEM,
        compiler_params=PARAMS,
        cost_estimate=pl.CostEstimate(
            flops=2 * tokens.shape[0] * D * COLS,
            bytes_accessed=tokens.size * 2,
            transcendentals=0,
        ),
        name="second_kernel",
    )(tokens, cotangents)


def add_kernel(left, right, out):
    out[...] = (left[...].astype(jnp.float32) + right[...].astype(jnp.float32)).astype(out.dtype)


def add(left, right):
    return pl.pallas_call(
        add_kernel,
        out_shape=NEAR_BLOCKS,
        in_specs=[VMEM, VMEM],
        out_specs=VMEM,
        compiler_params=PARAMS,
        name="add_kernel",
    )(left, right)


def sum_kernel(blocks, out, held):
    held[...] = blocks[...].astype(jnp.float32).sum(0)
    for index in range(N_FAR):
        out[index] = held[index * ROWS : (index + 1) * ROWS, :].astype(out.dtype)


def sum_near(blocks):
    return pl.pallas_call(
        sum_kernel,
        out_shape=FAR_BLOCKS,
        in_specs=[VMEM],
        out_specs=VMEM,
        scratch_shapes=[pltpu.VMEM((N_FAR * ROWS, COLS), jnp.float32)],
        compiler_params=PARAMS,
        name="sum_kernel",
    )(blocks)


def spread_kernel(blocks, out, held):
    for index in range(N_FAR):
        held[index * ROWS : (index + 1) * ROWS, :] = blocks[index].astype(jnp.float32)
    rows = held[...].astype(out.dtype)
    for index in range(N_NEAR):
        out[index] = rows


def spread_far(blocks):
    return pl.pallas_call(
        spread_kernel,
        out_shape=NEAR_BLOCKS,
        in_specs=[VMEM],
        out_specs=VMEM,
        scratch_shapes=[pltpu.VMEM((N_FAR * ROWS, COLS), jnp.float32)],
        compiler_params=PARAMS,
        name="spread_kernel",
    )(blocks)


def write_kernel(other, *refs):
    blocks, out, done = refs[0], refs[-2], refs[-1]
    core = lax.axis_index("core")
    bucket = 1 - core if other else core
    copies = []
    for x in range(4):
        for yp in range(2):
            copies.append(
                pltpu.make_async_copy(
                    blocks.at[x, yp], out.at[bucket, :, x, :, yp], done.at[x * 2 + yp]
                )
            )
            copies[-1].start()
    for copy in copies:
        copy.wait()


def write_bucket(blocks, other, out=None):
    shape = (2, 2, 4, 2, 2, BLOCK, COLS)
    whole = pl.BlockSpec(memory_space=pl.ANY)
    blocks = blocks.reshape(4, 2, 2, 2, BLOCK, COLS)
    return pl.pallas_call(
        functools.partial(write_kernel, other),
        out_shape=jax.ShapeDtypeStruct(shape, jnp.bfloat16),
        in_specs=[VMEM] if out is None else [VMEM, whole],
        out_specs=whole,
        scratch_shapes=[pltpu.SemaphoreType.DMA((N_NEAR,))],
        input_output_aliases={} if out is None else {1: 0},
        compiler_params=PARAMS,
        cost_estimate=pl.CostEstimate(flops=0, bytes_accessed=2 * D * COLS * 2, transcendentals=0),
        name="write_kernel",
    )(*([blocks] if out is None else [blocks, out]))


def adam(gradient, params, moment, second):
    new_moment = 0.9 * moment + 0.1 * gradient
    new_second = 0.95 * second + 0.05 * gradient * gradient
    first_fix = 1.0 - 0.9**10
    second_fix = 1.0 - 0.95**10
    update = new_moment / first_fix / (jnp.sqrt(new_second / second_fix) + 1e-08)
    new_params = params - 0.01 * (update + 0.1 * params)
    return new_params, new_moment, new_second


def finish_kernel(blocks, state, gradient, out):
    gradient[...] = blocks[...].astype(jnp.float32).sum(0)
    rounded = adam(gradient[...], state[0], state[1], state[2])[0].astype(out.dtype)
    for index in range(N_FAR):
        out[index] = rounded


def finish(blocks, state):
    return pl.pallas_call(
        finish_kernel,
        out_shape=[pltpu.VMEM((ROWS, COLS), jnp.float32), FAR_BLOCKS],
        in_specs=[VMEM, VMEM],
        out_specs=[VMEM, VMEM],
        compiler_params=PARAMS,
        name="finish_kernel",
    )(blocks, state)


def in_order(first, home, other, axis):
    return jnp.concatenate([jnp.where(first, home, other), jnp.where(first, other, home)], axis=axis)


def on_device(tokens, cotangents, params, moment, second):
    first = lax.axis_index("core") == 0

    away, tokens, cotangents = first_gradient(tokens, cotangents)
    away = lax.ppermute(away, "core", SWAP)
    home = second_gradient(tokens, cotangents)

    state = jnp.stack([params, moment, second], axis=1)
    state, home = lax.optimization_barrier((state, home))
    home_state = jnp.where(first, state[0], state[1])
    other_state = lax.ppermute(jnp.where(first, state[1], state[0]), "core", SWAP)
    held = in_order(first, home_state, other_state, 1)
    away, held = lax.optimization_barrier((away, held))

    near = sum_near(exchange(add(home, away), NEAR))
    gradient, rounded = finish(exchange(near, FAR), held)
    far = exchange(rounded, FAR)

    keep = jnp.where(first, gradient[:6], gradient[6:])
    other = lax.ppermute(jnp.where(first, gradient[6:], gradient[:6]), "core", SWAP)
    owned = in_order(first, keep[None], other[None], 0)
    new_params, new_moment, new_second = adam(owned, params, moment, second)
    far, new_params, new_moment, new_second = lax.optimization_barrier(
        (far, new_params, new_moment, new_second)
    )

    mine = exchange(spread_far(far), NEAR)
    theirs = lax.ppermute(mine, "core", SWAP)
    gathered = write_bucket(theirs, True, write_bucket(mine, False))
    return (new_params, new_moment, new_second, gathered.reshape(2, D, COLS))


def solution(mesh):
    fine = Mesh(mesh.devices.reshape(SIZES), ALL)
    rows = P(None, ALL, None)
    return jax.shard_map(
        on_device,
        mesh=fine,
        in_specs=(P(ALL, None), rows, rows, rows, rows),
        out_specs=(rows, rows, rows, P()),
        check_vma=False,
    )
```

```python
import functools

import jax
import jax.numpy as jnp
from jax import lax
from jax.experimental import pallas as pl
from jax.experimental.pallas import tpu as pltpu
from jax.sharding import Mesh
from jax.sharding import PartitionSpec as P

ALL = ("yh", "x", "yl", "yp", "z", "core")
SIZES = (2, 4, 2, 2, 12, 2)
NEAR = ("x", "yp")
FAR = ("yh", "yl", "z")
SWAP = [(0, 1), (1, 0)]
N_NEAR, N_FAR = 8, 48
D, COLS = 4608, 128
ROWS = 12
BLOCK = 144
STEP = 1152

VMEM = pl.BlockSpec(memory_space=pltpu.VMEM)
PARAMS = pltpu.CompilerParams(vmem_limit_bytes=24 * 2**20)
NEAR_BLOCKS = pltpu.VMEM((N_NEAR, N_FAR * ROWS, COLS), jnp.bfloat16)
FAR_BLOCKS = pltpu.VMEM((N_FAR, ROWS, COLS), jnp.bfloat16)


def exchange(blocks, axes):
    return lax.all_to_all(blocks, axes, 0, 0, tiled=True)


def place(block):
    yh, x, yl, yp = block // 16, block // 4 % 4, block // 2 % 2, block % 2
    return x * 2 + yp, (yh * 2 + yl) * BLOCK


def multiply(tokens, cotangent, out, columns):
    turned = cotangent.astype(jnp.float32).T.astype(jnp.bfloat16)
    for step in columns:
        product = jnp.dot(
            turned, tokens[:, step * STEP : (step + 1) * STEP], preferred_element_type=jnp.float32
        )
        rows = product.astype(out.dtype).T
        for part in range(STEP // BLOCK):
            chip, first = place(step * (STEP // BLOCK) + part)
            out[chip, first : first + BLOCK, :] = rows[part * BLOCK : (part + 1) * BLOCK, :]


def first_kernel(tokens, cotangents, out, held, small, arrived):
    other = 1 - lax.axis_index("core")
    copies = [pltpu.make_async_copy(cotangents, small, arrived.at[2])]
    for half in range(2):
        columns = (slice(None), pl.ds(half * (D // 2), D // 2))
        copies.append(
            pltpu.make_async_copy(tokens.at[columns], held.at[columns], arrived.at[half])
        )
    for copy in copies:
        copy.start()
    copies[0].wait()
    for half in range(2):
        copies[1 + half].wait()
        multiply(held, small[other], out, (2 * half, 2 * half + 1))


def second_kernel(tokens, cotangents, out):
    multiply(tokens, cotangents[lax.axis_index("core")], out, range(D // STEP))


def first_gradient(tokens, cotangents):
    return pl.pallas_call(
        first_kernel,
        out_shape=[
            NEAR_BLOCKS,
            pltpu.VMEM(tokens.shape, jnp.bfloat16),
            pltpu.VMEM(cotangents.shape, jnp.bfloat16),
        ],
        in_specs=[pl.BlockSpec(memory_space=pltpu.HBM)] * 2,
        out_specs=[VMEM] * 3,
        scratch_shapes=[pltpu.SemaphoreType.DMA((3,))],
        compiler_params=pltpu.CompilerParams(vmem_limit_bytes=55_000_000),
        name="first_kernel",
    )(tokens, cotangents)


def second_gradient(tokens, cotangents):
    return pl.pallas_call(
        second_kernel,
        out_shape=NEAR_BLOCKS,
        in_specs=[VMEM, VMEM],
        out_specs=VMEM,
        compiler_params=PARAMS,
        cost_estimate=pl.CostEstimate(
            flops=2 * tokens.shape[0] * D * COLS,
            bytes_accessed=tokens.size * 2,
            transcendentals=0,
        ),
        name="second_kernel",
    )(tokens, cotangents)


def add_kernel(left, right, out):
    out[...] = (left[...].astype(jnp.float32) + right[...].astype(jnp.float32)).astype(out.dtype)


def add(left, right):
    return pl.pallas_call(
        add_kernel,
        out_shape=NEAR_BLOCKS,
        in_specs=[VMEM, VMEM],
        out_specs=VMEM,
        compiler_params=PARAMS,
        name="add_kernel",
    )(left, right)


def sum_kernel(blocks, out, held):
    held[...] = blocks[...].astype(jnp.float32).sum(0)
    for index in range(N_FAR):
        out[index] = held[index * ROWS : (index + 1) * ROWS, :].astype(out.dtype)


def sum_near(blocks):
    return pl.pallas_call(
        sum_kernel,
        out_shape=FAR_BLOCKS,
        in_specs=[VMEM],
        out_specs=VMEM,
        scratch_shapes=[pltpu.VMEM((N_FAR * ROWS, COLS), jnp.float32)],
        compiler_params=PARAMS,
        name="sum_kernel",
    )(blocks)


def spread_kernel(blocks, out, held):
    for index in range(N_FAR):
        held[index * ROWS : (index + 1) * ROWS, :] = blocks[index].astype(jnp.float32)
    rows = held[...].astype(out.dtype)
    for index in range(N_NEAR):
        out[index] = rows


def spread_far(blocks):
    return pl.pallas_call(
        spread_kernel,
        out_shape=NEAR_BLOCKS,
        in_specs=[VMEM],
        out_specs=VMEM,
        scratch_shapes=[pltpu.VMEM((N_FAR * ROWS, COLS), jnp.float32)],
        compiler_params=PARAMS,
        name="spread_kernel",
    )(blocks)


def write_kernel(other, *refs):
    blocks, out, done = refs[0], refs[-2], refs[-1]
    core = lax.axis_index("core")
    bucket = 1 - core if other else core
    copies = []
    for x in range(4):
        for yp in range(2):
            copies.append(
                pltpu.make_async_copy(
                    blocks.at[x, yp], out.at[bucket, :, x, :, yp], done.at[x * 2 + yp]
                )
            )
            copies[-1].start()
    for copy in copies:
        copy.wait()


def write_bucket(blocks, other, out=None):
    shape = (2, 2, 4, 2, 2, BLOCK, COLS)
    whole = pl.BlockSpec(memory_space=pl.ANY)
    blocks = blocks.reshape(4, 2, 2, 2, BLOCK, COLS)
    return pl.pallas_call(
        functools.partial(write_kernel, other),
        out_shape=jax.ShapeDtypeStruct(shape, jnp.bfloat16),
        in_specs=[VMEM] if out is None else [VMEM, whole],
        out_specs=whole,
        scratch_shapes=[pltpu.SemaphoreType.DMA((N_NEAR,))],
        input_output_aliases={} if out is None else {1: 0},
        compiler_params=PARAMS,
        cost_estimate=pl.CostEstimate(flops=0, bytes_accessed=2 * D * COLS * 2, transcendentals=0),
        name="write_kernel",
    )(*([blocks] if out is None else [blocks, out]))


def adam(gradient, params, moment, second):
    new_moment = 0.9 * moment + 0.1 * gradient
    new_second = 0.95 * second + 0.05 * gradient * gradient
    first_fix = 1.0 - 0.9**10
    second_fix = 1.0 - 0.95**10
    update = new_moment / first_fix / (jnp.sqrt(new_second / second_fix) + 1e-08)
    new_params = params - 0.01 * (update + 0.1 * params)
    return new_params, new_moment, new_second


def finish_kernel(blocks, state, gradient, out):
    gradient[...] = blocks[...].astype(jnp.float32).sum(0)
    rounded = adam(gradient[...], state[0], state[1], state[2])[0].astype(out.dtype)
    for index in range(N_FAR):
        out[index] = rounded


def finish(blocks, state):
    return pl.pallas_call(
        finish_kernel,
        out_shape=[pltpu.VMEM((ROWS, COLS), jnp.float32), FAR_BLOCKS],
        in_specs=[VMEM, VMEM],
        out_specs=[VMEM, VMEM],
        compiler_params=PARAMS,
        name="finish_kernel",
    )(blocks, state)


def in_order(first, home, other, axis):
    return jnp.concatenate([jnp.where(first, home, other), jnp.where(first, other, home)], axis=axis)


def on_device(tokens, cotangents, params, moment, second):
    first = lax.axis_index("core") == 0

    away, tokens, cotangents = first_gradient(tokens, cotangents)
    away = lax.ppermute(away, "core", SWAP)
    near = sum_near(exchange(add(second_gradient(tokens, cotangents), away), NEAR))

    params, moment, second, near = lax.optimization_barrier((params, moment, second, near))
    state = jnp.stack([params, moment, second], axis=1)
    home_state = jnp.where(first, state[0], state[1])
    other_state = lax.ppermute(jnp.where(first, state[1], state[0]), "core", SWAP)
    held = in_order(first, home_state, other_state, 1)

    gradient, rounded = finish(exchange(near, FAR), held)
    far = exchange(rounded, FAR)

    keep = jnp.where(first, gradient[:6], gradient[6:])
    other = lax.ppermute(jnp.where(first, gradient[6:], gradient[:6]), "core", SWAP)
    near, other = lax.optimization_barrier((spread_far(far), other))

    mine = exchange(near, NEAR)
    mine, other = lax.optimization_barrier((mine, other))
    theirs = lax.ppermute(mine, "core", SWAP)
    owned = in_order(first, keep[None], other[None], 0)
    new_params, new_moment, new_second = adam(owned, params, moment, second)
    gathered = write_bucket(theirs, True, write_bucket(mine, False))
    return (new_params, new_moment, new_second, gathered.reshape(2, D, COLS))


def solution(mesh):
    fine = Mesh(mesh.devices.reshape(SIZES), ALL)
    rows = P(None, ALL, None)
    return jax.shard_map(
        on_device,
        mesh=fine,
        in_specs=(P(ALL, None), rows, rows, rows, rows),
        out_specs=(rows, rows, rows, P()),
        check_vma=False,
    )
```

```python
import functools

import jax
import jax.numpy as jnp
from jax import lax
from jax.experimental import pallas as pl
from jax.experimental.pallas import tpu as pltpu
from jax.sharding import Mesh
from jax.sharding import PartitionSpec as P

ALL = ("yh", "x", "yl", "yp", "z", "core")
SIZES = (2, 4, 2, 2, 12, 2)
NEAR = ("x", "yp")
FAR = ("yh", "yl", "z")
SWAP = [(0, 1), (1, 0)]
N_NEAR, N_FAR = 8, 48
D, COLS = 4608, 128
ROWS = 12
BLOCK = 144
STEP = 1152

VMEM = pl.BlockSpec(memory_space=pltpu.VMEM)
PARAMS = pltpu.CompilerParams(vmem_limit_bytes=24 * 2**20)
NEAR_BLOCKS = pltpu.VMEM((N_NEAR, N_FAR * ROWS, COLS), jnp.bfloat16)
FAR_BLOCKS = pltpu.VMEM((N_FAR, ROWS, COLS), jnp.bfloat16)


def exchange(blocks, axes):
    return lax.all_to_all(blocks, axes, 0, 0, tiled=True)


def place(block):
    yh, x, yl, yp = block // 16, block // 4 % 4, block // 2 % 2, block % 2
    return x * 2 + yp, (yh * 2 + yl) * BLOCK


def multiply(tokens, cotangent, out, columns):
    turned = cotangent.astype(jnp.float32).T.astype(jnp.bfloat16)
    for step in columns:
        product = jnp.dot(
            turned, tokens[:, step * STEP : (step + 1) * STEP], preferred_element_type=jnp.float32
        )
        rows = product.astype(out.dtype).T
        for part in range(STEP // BLOCK):
            chip, first = place(step * (STEP // BLOCK) + part)
            out[chip, first : first + BLOCK, :] = rows[part * BLOCK : (part + 1) * BLOCK, :]


def first_kernel(tokens, cotangents, out, held, small, arrived):
    other = 1 - lax.axis_index("core")
    copies = [pltpu.make_async_copy(cotangents, small, arrived.at[2])]
    for half in range(2):
        columns = (slice(None), pl.ds(half * (D // 2), D // 2))
        copies.append(
            pltpu.make_async_copy(tokens.at[columns], held.at[columns], arrived.at[half])
        )
    for copy in copies:
        copy.start()
    copies[0].wait()
    for half in range(2):
        copies[1 + half].wait()
        multiply(held, small[other], out, (2 * half, 2 * half + 1))


def second_kernel(tokens, cotangents, out):
    multiply(tokens, cotangents[lax.axis_index("core")], out, range(D // STEP))


def first_gradient(tokens, cotangents):
    return pl.pallas_call(
        first_kernel,
        out_shape=[
            NEAR_BLOCKS,
            pltpu.VMEM(tokens.shape, jnp.bfloat16),
            pltpu.VMEM(cotangents.shape, jnp.bfloat16),
        ],
        in_specs=[pl.BlockSpec(memory_space=pltpu.HBM)] * 2,
        out_specs=[VMEM] * 3,
        scratch_shapes=[pltpu.SemaphoreType.DMA((3,))],
        compiler_params=pltpu.CompilerParams(vmem_limit_bytes=55_000_000),
        name="first_kernel",
    )(tokens, cotangents)


def second_gradient(tokens, cotangents):
    return pl.pallas_call(
        second_kernel,
        out_shape=NEAR_BLOCKS,
        in_specs=[VMEM, VMEM],
        out_specs=VMEM,
        compiler_params=PARAMS,
        cost_estimate=pl.CostEstimate(
            flops=2 * tokens.shape[0] * D * COLS,
            bytes_accessed=tokens.size * 2,
            transcendentals=0,
        ),
        name="second_kernel",
    )(tokens, cotangents)


def add_kernel(left, right, out):
    out[...] = (left[...].astype(jnp.float32) + right[...].astype(jnp.float32)).astype(out.dtype)


def add(left, right):
    return pl.pallas_call(
        add_kernel,
        out_shape=NEAR_BLOCKS,
        in_specs=[VMEM, VMEM],
        out_specs=VMEM,
        compiler_params=PARAMS,
        name="add_kernel",
    )(left, right)


def sum_kernel(blocks, out, held):
    held[...] = blocks[...].astype(jnp.float32).sum(0)
    for index in range(N_FAR):
        out[index] = held[index * ROWS : (index + 1) * ROWS, :].astype(out.dtype)


def sum_near(blocks):
    return pl.pallas_call(
        sum_kernel,
        out_shape=FAR_BLOCKS,
        in_specs=[VMEM],
        out_specs=VMEM,
        scratch_shapes=[pltpu.VMEM((N_FAR * ROWS, COLS), jnp.float32)],
        compiler_params=PARAMS,
        name="sum_kernel",
    )(blocks)


def spread_kernel(blocks, out, held):
    for index in range(N_FAR):
        held[index * ROWS : (index + 1) * ROWS, :] = blocks[index].astype(jnp.float32)
    rows = held[...].astype(out.dtype)
    for index in range(N_NEAR):
        out[index] = rows


def spread_far(blocks):
    return pl.pallas_call(
        spread_kernel,
        out_shape=NEAR_BLOCKS,
        in_specs=[VMEM],
        out_specs=VMEM,
        scratch_shapes=[pltpu.VMEM((N_FAR * ROWS, COLS), jnp.float32)],
        compiler_params=PARAMS,
        name="spread_kernel",
    )(blocks)


def write_kernel(other, *refs):
    blocks, out, done = refs[0], refs[-2], refs[-1]
    core = lax.axis_index("core")
    bucket = 1 - core if other else core
    copies = []
    for x in range(4):
        for yp in range(2):
            copies.append(
                pltpu.make_async_copy(
                    blocks.at[x, yp], out.at[bucket, :, x, :, yp], done.at[x * 2 + yp]
                )
            )
            copies[-1].start()
    for copy in copies:
        copy.wait()


def write_bucket(blocks, other, out=None):
    shape = (2, 2, 4, 2, 2, BLOCK, COLS)
    whole = pl.BlockSpec(memory_space=pl.ANY)
    blocks = blocks.reshape(4, 2, 2, 2, BLOCK, COLS)
    return pl.pallas_call(
        functools.partial(write_kernel, other),
        out_shape=jax.ShapeDtypeStruct(shape, jnp.bfloat16),
        in_specs=[VMEM] if out is None else [VMEM, whole],
        out_specs=whole,
        scratch_shapes=[pltpu.SemaphoreType.DMA((N_NEAR,))],
        input_output_aliases={} if out is None else {1: 0},
        compiler_params=PARAMS,
        cost_estimate=pl.CostEstimate(flops=0, bytes_accessed=2 * D * COLS * 2, transcendentals=0),
        name="write_kernel",
    )(*([blocks] if out is None else [blocks, out]))


def adam(gradient, params, moment, second):
    new_moment = 0.9 * moment + 0.1 * gradient
    new_second = 0.95 * second + 0.05 * gradient * gradient
    first_fix = 1.0 - 0.9**10
    second_fix = 1.0 - 0.95**10
    update = new_moment / first_fix / (jnp.sqrt(new_second / second_fix) + 1e-08)
    new_params = params - 0.01 * (update + 0.1 * params)
    return new_params, new_moment, new_second


def finish_kernel(blocks, state, gradient, out):
    gradient[...] = blocks[...].astype(jnp.float32).sum(0)
    rounded = adam(gradient[...], state[0], state[1], state[2])[0].astype(out.dtype)
    for index in range(N_FAR):
        out[index] = rounded


def finish(blocks, state):
    return pl.pallas_call(
        finish_kernel,
        out_shape=[pltpu.VMEM((ROWS, COLS), jnp.float32), FAR_BLOCKS],
        in_specs=[VMEM, VMEM],
        out_specs=[VMEM, VMEM],
        compiler_params=PARAMS,
        name="finish_kernel",
    )(blocks, state)


def in_order(first, home, other, axis):
    return jnp.concatenate([jnp.where(first, home, other), jnp.where(first, other, home)], axis=axis)


def on_device(tokens, cotangents, params, moment, second):
    first = lax.axis_index("core") == 0

    away, tokens, cotangents = first_gradient(tokens, cotangents)
    away = lax.ppermute(away, "core", SWAP)
    home = second_gradient(tokens, cotangents)
    params, moment, second, home = lax.optimization_barrier((params, moment, second, home))
    state = jnp.stack([params, moment, second], axis=1)
    home_state = jnp.where(first, state[0], state[1])
    other_state = jnp.where(first, state[1], state[0])
    home_state, other_state, away = lax.optimization_barrier((home_state, other_state, away))
    near = sum_near(exchange(add(home, away), NEAR))

    other_state, near = lax.optimization_barrier((other_state, near))
    other_state = lax.ppermute(other_state, "core", SWAP)
    held = in_order(first, home_state, other_state, 1)

    gradient, rounded = finish(exchange(near, FAR), held)
    far = exchange(rounded, FAR)

    keep = jnp.where(first, gradient[:6], gradient[6:])
    other = lax.ppermute(jnp.where(first, gradient[6:], gradient[:6]), "core", SWAP)
    near, other = lax.optimization_barrier((spread_far(far), other))

    mine = exchange(near, NEAR)
    mine, other = lax.optimization_barrier((mine, other))
    theirs = lax.ppermute(mine, "core", SWAP)
    owned = in_order(first, keep[None], other[None], 0)
    new_params, new_moment, new_second = adam(owned, params, moment, second)
    gathered = write_bucket(theirs, True, write_bucket(mine, False))
    return (new_params, new_moment, new_second, gathered.reshape(2, D, COLS))


def solution(mesh):
    fine = Mesh(mesh.devices.reshape(SIZES), ALL)
    rows = P(None, ALL, None)
    return jax.shard_map(
        on_device,
        mesh=fine,
        in_specs=(P(ALL, None), rows, rows, rows, rows),
        out_specs=(rows, rows, rows, P()),
        check_vma=False,
    )
```

```python
import functools

import jax
import jax.numpy as jnp
from jax import lax
from jax.experimental import pallas as pl
from jax.experimental.pallas import tpu as pltpu
from jax.sharding import Mesh
from jax.sharding import PartitionSpec as P

ALL = ("yh", "x", "yl", "yp", "z", "core")
SIZES = (2, 4, 2, 2, 12, 2)
NEAR = ("x", "yp")
FAR = ("yl", "z", "yh")
SWAP = [(0, 1), (1, 0)]
N_NEAR, N_FAR = 8, 48
D, COLS = 4608, 128
ROWS = 12
BLOCK = 144
STEP = 1152
FETCHES = ((0, 3), (3, 4))

VMEM = pl.BlockSpec(memory_space=pltpu.VMEM)
PARAMS = pltpu.CompilerParams(vmem_limit_bytes=24 * 2**20)
NEAR_BLOCKS = pltpu.VMEM((N_NEAR, N_FAR * ROWS, COLS), jnp.bfloat16)
FAR_BLOCKS = pltpu.VMEM((N_FAR, ROWS, COLS), jnp.bfloat16)


def exchange(blocks, axes):
    return lax.all_to_all(blocks, axes, 0, 0, tiled=True)


def place(block):
    yh, x, yl, yp = block // 16, block // 4 % 4, block // 2 % 2, block % 2
    return x * 2 + yp, (yh * 2 + yl) * BLOCK


def far_rows(index):
    yl, z, yh = index // 24, index // 2 % 12, index % 2
    first = ((yh * 2 + yl) * 12 + z) * ROWS
    return slice(first, first + ROWS)


def multiply(tokens, cotangent, out, columns):
    turned = cotangent.astype(jnp.float32).T.astype(jnp.bfloat16)
    for step in columns:
        product = jnp.dot(
            turned, tokens[:, step * STEP : (step + 1) * STEP], preferred_element_type=jnp.float32
        )
        rows = product.astype(out.dtype).T
        for part in range(STEP // BLOCK):
            chip, first = place(step * (STEP // BLOCK) + part)
            out[chip, first : first + BLOCK, :] = rows[part * BLOCK : (part + 1) * BLOCK, :]


def first_kernel(tokens, cotangents, out, held, small, arrived):
    other = 1 - lax.axis_index("core")
    copies = [pltpu.make_async_copy(cotangents, small, arrived.at[2])]
    for index, (first, last) in enumerate(FETCHES):
        columns = (slice(None), pl.ds(first * STEP, (last - first) * STEP))
        copies.append(
            pltpu.make_async_copy(tokens.at[columns], held.at[columns], arrived.at[index])
        )
    for copy in copies:
        copy.start()
    copies[0].wait()
    for copy, (first, last) in zip(copies[1:], FETCHES):
        copy.wait()
        multiply(held, small[other], out, range(first, last))


def second_kernel(tokens, cotangents, out):
    multiply(tokens, cotangents[lax.axis_index("core")], out, range(D // STEP))


def first_gradient(tokens, cotangents):
    return pl.pallas_call(
        first_kernel,
        out_shape=[
            NEAR_BLOCKS,
            pltpu.VMEM(tokens.shape, jnp.bfloat16),
            pltpu.VMEM(cotangents.shape, jnp.bfloat16),
        ],
        in_specs=[pl.BlockSpec(memory_space=pltpu.HBM)] * 2,
        out_specs=[VMEM] * 3,
        scratch_shapes=[pltpu.SemaphoreType.DMA((3,))],
        compiler_params=pltpu.CompilerParams(vmem_limit_bytes=55_000_000),
        name="first_kernel",
    )(tokens, cotangents)


def second_gradient(tokens, cotangents):
    return pl.pallas_call(
        second_kernel,
        out_shape=NEAR_BLOCKS,
        in_specs=[VMEM, VMEM],
        out_specs=VMEM,
        compiler_params=PARAMS,
        cost_estimate=pl.CostEstimate(
            flops=2 * tokens.shape[0] * D * COLS,
            bytes_accessed=tokens.size * 2,
            transcendentals=0,
        ),
        name="second_kernel",
    )(tokens, cotangents)


def add_kernel(left, right, out):
    out[...] = (left[...].astype(jnp.float32) + right[...].astype(jnp.float32)).astype(out.dtype)


def add(left, right):
    return pl.pallas_call(
        add_kernel,
        out_shape=NEAR_BLOCKS,
        in_specs=[VMEM, VMEM],
        out_specs=VMEM,
        compiler_params=PARAMS,
        name="add_kernel",
    )(left, right)


def sum_kernel(blocks, out, held):
    held[...] = blocks[...].astype(jnp.float32).sum(0)
    for index in range(N_FAR):
        out[index] = held[far_rows(index), :].astype(out.dtype)


def sum_near(blocks):
    return pl.pallas_call(
        sum_kernel,
        out_shape=FAR_BLOCKS,
        in_specs=[VMEM],
        out_specs=VMEM,
        scratch_shapes=[pltpu.VMEM((N_FAR * ROWS, COLS), jnp.float32)],
        compiler_params=PARAMS,
        name="sum_kernel",
    )(blocks)


def spread_kernel(blocks, out, held):
    for index in range(N_FAR):
        held[far_rows(index), :] = blocks[index].astype(jnp.float32)
    rows = held[...].astype(out.dtype)
    for index in range(N_NEAR):
        out[index] = rows


def spread_far(blocks):
    return pl.pallas_call(
        spread_kernel,
        out_shape=NEAR_BLOCKS,
        in_specs=[VMEM],
        out_specs=VMEM,
        scratch_shapes=[pltpu.VMEM((N_FAR * ROWS, COLS), jnp.float32)],
        compiler_params=PARAMS,
        name="spread_kernel",
    )(blocks)


def write_kernel(other, *refs):
    blocks, out, done = refs[0], refs[-2], refs[-1]
    core = lax.axis_index("core")
    bucket = 1 - core if other else core
    copies = []
    for x in range(4):
        for yp in range(2):
            copies.append(
                pltpu.make_async_copy(
                    blocks.at[x, yp], out.at[bucket, :, x, :, yp], done.at[x * 2 + yp]
                )
            )
            copies[-1].start()
    for copy in copies:
        copy.wait()


def write_bucket(blocks, other, out=None):
    shape = (2, 2, 4, 2, 2, BLOCK, COLS)
    whole = pl.BlockSpec(memory_space=pl.ANY)
    blocks = blocks.reshape(4, 2, 2, 2, BLOCK, COLS)
    return pl.pallas_call(
        functools.partial(write_kernel, other),
        out_shape=jax.ShapeDtypeStruct(shape, jnp.bfloat16),
        in_specs=[VMEM] if out is None else [VMEM, whole],
        out_specs=whole,
        scratch_shapes=[pltpu.SemaphoreType.DMA((N_NEAR,))],
        input_output_aliases={} if out is None else {1: 0},
        compiler_params=PARAMS,
        cost_estimate=pl.CostEstimate(flops=0, bytes_accessed=2 * D * COLS * 2, transcendentals=0),
        name="write_kernel",
    )(*([blocks] if out is None else [blocks, out]))


def adam(gradient, params, moment, second):
    new_moment = 0.9 * moment + 0.1 * gradient
    new_second = 0.95 * second + 0.05 * gradient * gradient
    first_fix = 1.0 - 0.9**10
    second_fix = 1.0 - 0.95**10
    update = new_moment / first_fix / (jnp.sqrt(new_second / second_fix) + 1e-08)
    new_params = params - 0.01 * (update + 0.1 * params)
    return new_params, new_moment, new_second


def finish_kernel(blocks, state, gradient, out):
    gradient[...] = blocks[...].astype(jnp.float32).sum(0)
    rounded = adam(gradient[...], state[0], state[1], state[2])[0].astype(out.dtype)
    for index in range(N_FAR):
        out[index] = rounded


def finish(blocks, state):
    return pl.pallas_call(
        finish_kernel,
        out_shape=[pltpu.VMEM((ROWS, COLS), jnp.float32), FAR_BLOCKS],
        in_specs=[VMEM, VMEM],
        out_specs=[VMEM, VMEM],
        compiler_params=PARAMS,
        name="finish_kernel",
    )(blocks, state)


def in_order(first, home, other, axis):
    return jnp.concatenate([jnp.where(first, home, other), jnp.where(first, other, home)], axis=axis)


def on_device(tokens, cotangents, params, moment, second):
    first = lax.axis_index("core") == 0

    away, tokens, cotangents = first_gradient(tokens, cotangents)
    away = lax.ppermute(away, "core", SWAP)
    home = second_gradient(tokens, cotangents)
    params, moment, second, home = lax.optimization_barrier((params, moment, second, home))
    state = jnp.stack([params, moment, second], axis=1)
    home_state = jnp.where(first, state[0], state[1])
    other_state = jnp.where(first, state[1], state[0])
    home_state, other_state, away = lax.optimization_barrier((home_state, other_state, away))
    near = sum_near(exchange(add(home, away), NEAR))

    other_state, near = lax.optimization_barrier((other_state, near))
    other_state = lax.ppermute(other_state, "core", SWAP)
    held = in_order(first, home_state, other_state, 1)

    gradient, rounded = finish(exchange(near, FAR), held)
    far = exchange(rounded, FAR)

    keep = jnp.where(first, gradient[:6], gradient[6:])
    other = lax.ppermute(jnp.where(first, gradient[6:], gradient[:6]), "core", SWAP)
    near, other = lax.optimization_barrier((spread_far(far), other))

    mine = exchange(near, NEAR)
    mine, other = lax.optimization_barrier((mine, other))
    theirs = lax.ppermute(mine, "core", SWAP)
    owned = in_order(first, keep[None], other[None], 0)
    new_params, new_moment, new_second = adam(owned, params, moment, second)
    gathered = write_bucket(theirs, True, write_bucket(mine, False))
    return (new_params, new_moment, new_second, gathered.reshape(2, D, COLS))


def solution(mesh):
    fine = Mesh(mesh.devices.reshape(SIZES), ALL)
    rows = P(None, ALL, None)
    return jax.shard_map(
        on_device,
        mesh=fine,
        in_specs=(P(ALL, None), rows, rows, rows, rows),
        out_specs=(rows, rows, rows, P()),
        check_vma=False,
    )
```

```python
import functools

import jax
import jax.numpy as jnp
from jax import lax
from jax.experimental import pallas as pl
from jax.experimental.pallas import tpu as pltpu
from jax.sharding import Mesh
from jax.sharding import PartitionSpec as P

ALL = ("yh", "x", "yl", "yp", "z", "core")
SIZES = (2, 4, 2, 2, 12, 2)
NEAR = ("x", "yp")
FAR = ("yl", "z", "yh")
SWAP = [(0, 1), (1, 0)]
N_NEAR, N_FAR = 8, 48
D, COLS = 4608, 128
ROWS = 12
BLOCK = 144
STEP = 1152
FETCHES = ((0, 2), (2, 4))

VMEM = pl.BlockSpec(memory_space=pltpu.VMEM)
PARAMS = pltpu.CompilerParams(vmem_limit_bytes=24 * 2**20)
NEAR_BLOCKS = pltpu.VMEM((N_NEAR, N_FAR * ROWS, COLS), jnp.bfloat16)
FAR_BLOCKS = pltpu.VMEM((N_FAR, ROWS, COLS), jnp.bfloat16)


def exchange(blocks, axes):
    return lax.all_to_all(blocks, axes, 0, 0, tiled=True)


def place(block):
    yh, x, yl, yp = block // 16, block // 4 % 4, block // 2 % 2, block % 2
    return x * 2 + yp, (yh * 2 + yl) * BLOCK


def far_rows(index):
    yl, z, yh = index // 24, index // 2 % 12, index % 2
    first = ((yh * 2 + yl) * 12 + z) * ROWS
    return slice(first, first + ROWS)


def multiply(tokens, cotangent, out, columns):
    turned = cotangent.astype(jnp.float32).T.astype(jnp.bfloat16)
    for step in columns:
        product = jnp.dot(
            turned, tokens[:, step * STEP : (step + 1) * STEP], preferred_element_type=jnp.float32
        )
        rows = product.astype(out.dtype).T
        for part in range(STEP // BLOCK):
            chip, first = place(step * (STEP // BLOCK) + part)
            out[chip, first : first + BLOCK, :] = rows[part * BLOCK : (part + 1) * BLOCK, :]


def first_kernel(tokens, cotangents, out, held, small, arrived):
    other = 1 - lax.axis_index("core")
    copies = [pltpu.make_async_copy(cotangents, small, arrived.at[2])]
    for index, (first, last) in enumerate(FETCHES):
        columns = (slice(None), pl.ds(first * STEP, (last - first) * STEP))
        copies.append(
            pltpu.make_async_copy(tokens.at[columns], held.at[columns], arrived.at[index])
        )
    for copy in copies:
        copy.start()
    copies[0].wait()
    for copy, (first, last) in zip(copies[1:], FETCHES):
        copy.wait()
        multiply(held, small[other], out, range(first, last))


def second_kernel(tokens, cotangents, out):
    multiply(tokens, cotangents[lax.axis_index("core")], out, range(D // STEP))


def first_gradient(tokens, cotangents):
    return pl.pallas_call(
        first_kernel,
        out_shape=[
            NEAR_BLOCKS,
            pltpu.VMEM(tokens.shape, jnp.bfloat16),
            pltpu.VMEM(cotangents.shape, jnp.bfloat16),
        ],
        in_specs=[pl.BlockSpec(memory_space=pltpu.HBM)] * 2,
        out_specs=[VMEM] * 3,
        scratch_shapes=[pltpu.SemaphoreType.DMA((3,))],
        compiler_params=pltpu.CompilerParams(vmem_limit_bytes=55_000_000),
        name="first_kernel",
    )(tokens, cotangents)


def second_gradient(tokens, cotangents):
    return pl.pallas_call(
        second_kernel,
        out_shape=NEAR_BLOCKS,
        in_specs=[VMEM, VMEM],
        out_specs=VMEM,
        compiler_params=PARAMS,
        cost_estimate=pl.CostEstimate(
            flops=2 * tokens.shape[0] * D * COLS,
            bytes_accessed=tokens.size * 2,
            transcendentals=0,
        ),
        name="second_kernel",
    )(tokens, cotangents)


def add_kernel(left, right, out):
    out[...] = (left[...].astype(jnp.float32) + right[...].astype(jnp.float32)).astype(out.dtype)


def add(left, right):
    return pl.pallas_call(
        add_kernel,
        out_shape=NEAR_BLOCKS,
        in_specs=[VMEM, VMEM],
        out_specs=VMEM,
        compiler_params=PARAMS,
        name="add_kernel",
    )(left, right)


def sum_kernel(blocks, out, held):
    held[...] = blocks[...].astype(jnp.float32).sum(0)
    for index in range(N_FAR):
        out[index] = held[far_rows(index), :].astype(out.dtype)


def sum_near(blocks):
    return pl.pallas_call(
        sum_kernel,
        out_shape=FAR_BLOCKS,
        in_specs=[VMEM],
        out_specs=VMEM,
        scratch_shapes=[pltpu.VMEM((N_FAR * ROWS, COLS), jnp.float32)],
        compiler_params=PARAMS,
        name="sum_kernel",
    )(blocks)


def spread_kernel(blocks, out, held):
    for index in range(N_FAR):
        held[far_rows(index), :] = blocks[index].astype(jnp.float32)
    rows = held[...].astype(out.dtype)
    for index in range(N_NEAR):
        out[index] = rows


def spread_far(blocks):
    return pl.pallas_call(
        spread_kernel,
        out_shape=NEAR_BLOCKS,
        in_specs=[VMEM],
        out_specs=VMEM,
        scratch_shapes=[pltpu.VMEM((N_FAR * ROWS, COLS), jnp.float32)],
        compiler_params=PARAMS,
        name="spread_kernel",
    )(blocks)


def write_kernel(other, *refs):
    blocks, out, done = refs[0], refs[-2], refs[-1]
    core = lax.axis_index("core")
    bucket = 1 - core if other else core
    copies = []
    for x in range(4):
        for yp in range(2):
            copies.append(
                pltpu.make_async_copy(
                    blocks.at[x, yp], out.at[bucket, :, x, :, yp], done.at[x * 2 + yp]
                )
            )
            copies[-1].start()
    for copy in copies:
        copy.wait()


def write_bucket(blocks, other, out=None):
    shape = (2, 2, 4, 2, 2, BLOCK, COLS)
    whole = pl.BlockSpec(memory_space=pl.ANY)
    blocks = blocks.reshape(4, 2, 2, 2, BLOCK, COLS)
    return pl.pallas_call(
        functools.partial(write_kernel, other),
        out_shape=jax.ShapeDtypeStruct(shape, jnp.bfloat16),
        in_specs=[VMEM] if out is None else [VMEM, whole],
        out_specs=whole,
        scratch_shapes=[pltpu.SemaphoreType.DMA((N_NEAR,))],
        input_output_aliases={} if out is None else {1: 0},
        compiler_params=PARAMS,
        cost_estimate=pl.CostEstimate(flops=0, bytes_accessed=2 * D * COLS * 2, transcendentals=0),
        name="write_kernel",
    )(*([blocks] if out is None else [blocks, out]))


def adam(gradient, params, moment, second):
    new_moment = 0.9 * moment + 0.1 * gradient
    new_second = 0.95 * second + 0.05 * gradient * gradient
    first_fix = 1.0 - 0.9**10
    second_fix = 1.0 - 0.95**10
    update = new_moment / first_fix / (jnp.sqrt(new_second / second_fix) + 1e-08)
    new_params = params - 0.01 * (update + 0.1 * params)
    return new_params, new_moment, new_second


def finish_kernel(blocks, state, gradient, out):
    gradient[...] = blocks[...].astype(jnp.float32).sum(0)
    rounded = adam(gradient[...], state[0], state[1], state[2])[0].astype(out.dtype)
    for index in range(N_FAR):
        out[index] = rounded


def finish(blocks, state):
    return pl.pallas_call(
        finish_kernel,
        out_shape=[pltpu.VMEM((ROWS, COLS), jnp.float32), FAR_BLOCKS],
        in_specs=[VMEM, VMEM],
        out_specs=[VMEM, VMEM],
        compiler_params=PARAMS,
        name="finish_kernel",
    )(blocks, state)


def in_order(first, home, other, axis):
    return jnp.concatenate([jnp.where(first, home, other), jnp.where(first, other, home)], axis=axis)


def on_device(tokens, cotangents, params, moment, second):
    first = lax.axis_index("core") == 0

    away, tokens, cotangents = first_gradient(tokens, cotangents)
    away = lax.ppermute(away, "core", SWAP)
    home = second_gradient(tokens, cotangents)
    params, moment, second, home = lax.optimization_barrier((params, moment, second, home))
    state = jnp.stack([params, moment, second], axis=1)
    home_state = jnp.where(first, state[0], state[1])
    other_state = jnp.where(first, state[1], state[0])
    home_state, other_state, away = lax.optimization_barrier((home_state, other_state, away))
    near = sum_near(exchange(add(home, away), NEAR))

    other_state, near = lax.optimization_barrier((other_state, near))
    other_state = lax.ppermute(other_state, "core", SWAP)
    held = in_order(first, home_state, other_state, 1)

    gradient, rounded = finish(exchange(near, FAR), held)
    far = exchange(rounded, FAR)

    keep = jnp.where(first, gradient[:6], gradient[6:])
    other = lax.ppermute(jnp.where(first, gradient[6:], gradient[:6]), "core", SWAP)
    near, other = lax.optimization_barrier((spread_far(far), other))

    mine = exchange(near, NEAR)
    mine, other = lax.optimization_barrier((mine, other))
    theirs = lax.ppermute(mine, "core", SWAP)
    owned = in_order(first, keep[None], other[None], 0)
    new_params, new_moment, new_second = adam(owned, params, moment, second)
    gathered = write_bucket(theirs, True, write_bucket(mine, False))
    return (new_params, new_moment, new_second, gathered.reshape(2, D, COLS))


def solution(mesh):
    fine = Mesh(mesh.devices.reshape(SIZES), ALL)
    rows = P(None, ALL, None)
    return jax.shard_map(
        on_device,
        mesh=fine,
        in_specs=(P(ALL, None), rows, rows, rows, rows),
        out_specs=(rows, rows, rows, P()),
        check_vma=False,
    )
```

```python
import functools

import jax
import jax.numpy as jnp
from jax import lax
from jax.experimental import pallas as pl
from jax.experimental.pallas import tpu as pltpu
from jax.sharding import Mesh
from jax.sharding import PartitionSpec as P

ALL = ("yh", "x", "yl", "yp", "z", "core")
SIZES = (2, 4, 2, 2, 12, 2)
NEAR = ("yp", "x")
FAR = ("yl", "z", "yh")
SWAP = [(0, 1), (1, 0)]
N_NEAR, N_FAR = 8, 48
D, COLS = 4608, 128
ROWS = 12
BLOCK = 144
STEP = 1152
FETCHES = ((0, 2), (2, 4))

VMEM = pl.BlockSpec(memory_space=pltpu.VMEM)
PARAMS = pltpu.CompilerParams(vmem_limit_bytes=24 * 2**20)
NEAR_BLOCKS = pltpu.VMEM((N_NEAR, N_FAR * ROWS, COLS), jnp.bfloat16)
FAR_BLOCKS = pltpu.VMEM((N_FAR, ROWS, COLS), jnp.bfloat16)


def exchange(blocks, axes):
    return lax.all_to_all(blocks, axes, 0, 0, tiled=True)


def place(block):
    yh, x, yl, yp = block // 16, block // 4 % 4, block // 2 % 2, block % 2
    return yp * 4 + x, (yh * 2 + yl) * BLOCK


def far_rows(index):
    yl, z, yh = index // 24, index // 2 % 12, index % 2
    first = ((yh * 2 + yl) * 12 + z) * ROWS
    return slice(first, first + ROWS)


def multiply(tokens, cotangent, out, columns):
    turned = cotangent.astype(jnp.float32).T.astype(jnp.bfloat16)
    for step in columns:
        product = jnp.dot(
            turned, tokens[:, step * STEP : (step + 1) * STEP], preferred_element_type=jnp.float32
        )
        rows = product.astype(out.dtype).T
        for part in range(STEP // BLOCK):
            chip, first = place(step * (STEP // BLOCK) + part)
            out[chip, first : first + BLOCK, :] = rows[part * BLOCK : (part + 1) * BLOCK, :]


def first_kernel(tokens, cotangents, out, held, small, arrived):
    other = 1 - lax.axis_index("core")
    copies = [pltpu.make_async_copy(cotangents, small, arrived.at[2])]
    for index, (first, last) in enumerate(FETCHES):
        columns = (slice(None), pl.ds(first * STEP, (last - first) * STEP))
        copies.append(
            pltpu.make_async_copy(tokens.at[columns], held.at[columns], arrived.at[index])
        )
    for copy in copies:
        copy.start()
    copies[0].wait()
    for copy, (first, last) in zip(copies[1:], FETCHES):
        copy.wait()
        multiply(held, small[other], out, range(first, last))


def second_kernel(tokens, cotangents, out):
    multiply(tokens, cotangents[lax.axis_index("core")], out, range(D // STEP))


def first_gradient(tokens, cotangents):
    return pl.pallas_call(
        first_kernel,
        out_shape=[
            NEAR_BLOCKS,
            pltpu.VMEM(tokens.shape, jnp.bfloat16),
            pltpu.VMEM(cotangents.shape, jnp.bfloat16),
        ],
        in_specs=[pl.BlockSpec(memory_space=pltpu.HBM)] * 2,
        out_specs=[VMEM] * 3,
        scratch_shapes=[pltpu.SemaphoreType.DMA((3,))],
        compiler_params=pltpu.CompilerParams(vmem_limit_bytes=55_000_000),
        name="first_kernel",
    )(tokens, cotangents)


def second_gradient(tokens, cotangents):
    return pl.pallas_call(
        second_kernel,
        out_shape=NEAR_BLOCKS,
        in_specs=[VMEM, VMEM],
        out_specs=VMEM,
        compiler_params=PARAMS,
        cost_estimate=pl.CostEstimate(
            flops=2 * tokens.shape[0] * D * COLS,
            bytes_accessed=tokens.size * 2,
            transcendentals=0,
        ),
        name="second_kernel",
    )(tokens, cotangents)


def add_kernel(left, right, out):
    out[...] = (left[...].astype(jnp.float32) + right[...].astype(jnp.float32)).astype(out.dtype)


def add(left, right):
    return pl.pallas_call(
        add_kernel,
        out_shape=NEAR_BLOCKS,
        in_specs=[VMEM, VMEM],
        out_specs=VMEM,
        compiler_params=PARAMS,
        name="add_kernel",
    )(left, right)


def sum_kernel(blocks, out, held):
    held[...] = blocks[...].astype(jnp.float32).sum(0)
    for index in range(N_FAR):
        out[index] = held[far_rows(index), :].astype(out.dtype)


def sum_near(blocks):
    return pl.pallas_call(
        sum_kernel,
        out_shape=FAR_BLOCKS,
        in_specs=[VMEM],
        out_specs=VMEM,
        scratch_shapes=[pltpu.VMEM((N_FAR * ROWS, COLS), jnp.float32)],
        compiler_params=PARAMS,
        name="sum_kernel",
    )(blocks)


def spread_kernel(blocks, out, held):
    for index in range(N_FAR):
        held[far_rows(index), :] = blocks[index].astype(jnp.float32)
    rows = held[...].astype(out.dtype)
    for index in range(N_NEAR):
        out[index] = rows


def spread_far(blocks):
    return pl.pallas_call(
        spread_kernel,
        out_shape=NEAR_BLOCKS,
        in_specs=[VMEM],
        out_specs=VMEM,
        scratch_shapes=[pltpu.VMEM((N_FAR * ROWS, COLS), jnp.float32)],
        compiler_params=PARAMS,
        name="spread_kernel",
    )(blocks)


def write_kernel(other, *refs):
    blocks, out, done = refs[0], refs[-2], refs[-1]
    core = lax.axis_index("core")
    bucket = 1 - core if other else core
    copies = []
    for x in range(4):
        for yp in range(2):
            copies.append(
                pltpu.make_async_copy(
                    blocks.at[yp, x], out.at[bucket, :, x, :, yp], done.at[yp * 4 + x]
                )
            )
            copies[-1].start()
    for copy in copies:
        copy.wait()


def write_bucket(blocks, other, out=None):
    shape = (2, 2, 4, 2, 2, BLOCK, COLS)
    whole = pl.BlockSpec(memory_space=pl.ANY)
    blocks = blocks.reshape(2, 4, 2, 2, BLOCK, COLS)
    return pl.pallas_call(
        functools.partial(write_kernel, other),
        out_shape=jax.ShapeDtypeStruct(shape, jnp.bfloat16),
        in_specs=[VMEM] if out is None else [VMEM, whole],
        out_specs=whole,
        scratch_shapes=[pltpu.SemaphoreType.DMA((N_NEAR,))],
        input_output_aliases={} if out is None else {1: 0},
        compiler_params=PARAMS,
        cost_estimate=pl.CostEstimate(flops=0, bytes_accessed=2 * D * COLS * 2, transcendentals=0),
        name="write_kernel",
    )(*([blocks] if out is None else [blocks, out]))


def adam(gradient, params, moment, second):
    new_moment = 0.9 * moment + 0.1 * gradient
    new_second = 0.95 * second + 0.05 * gradient * gradient
    first_fix = 1.0 - 0.9**10
    second_fix = 1.0 - 0.95**10
    update = new_moment / first_fix / (jnp.sqrt(new_second / second_fix) + 1e-08)
    new_params = params - 0.01 * (update + 0.1 * params)
    return new_params, new_moment, new_second


def finish_kernel(blocks, state, gradient, out):
    gradient[...] = blocks[...].astype(jnp.float32).sum(0)
    rounded = adam(gradient[...], state[0], state[1], state[2])[0].astype(out.dtype)
    for index in range(N_FAR):
        out[index] = rounded


def finish(blocks, state):
    return pl.pallas_call(
        finish_kernel,
        out_shape=[pltpu.VMEM((ROWS, COLS), jnp.float32), FAR_BLOCKS],
        in_specs=[VMEM, VMEM],
        out_specs=[VMEM, VMEM],
        compiler_params=PARAMS,
        name="finish_kernel",
    )(blocks, state)


def in_order(first, home, other, axis):
    return jnp.concatenate([jnp.where(first, home, other), jnp.where(first, other, home)], axis=axis)


def on_device(tokens, cotangents, params, moment, second):
    first = lax.axis_index("core") == 0

    away, tokens, cotangents = first_gradient(tokens, cotangents)
    away = lax.ppermute(away, "core", SWAP)
    home = second_gradient(tokens, cotangents)
    params, moment, second, home = lax.optimization_barrier((params, moment, second, home))
    state = jnp.stack([params, moment, second], axis=1)
    home_state = jnp.where(first, state[0], state[1])
    other_state = jnp.where(first, state[1], state[0])
    home_state, other_state, away = lax.optimization_barrier((home_state, other_state, away))
    near = sum_near(exchange(add(home, away), NEAR))

    other_state, near = lax.optimization_barrier((other_state, near))
    other_state = lax.ppermute(other_state, "core", SWAP)
    held = in_order(first, home_state, other_state, 1)

    gradient, rounded = finish(exchange(near, FAR), held)
    far = exchange(rounded, FAR)

    keep = jnp.where(first, gradient[:6], gradient[6:])
    other = lax.ppermute(jnp.where(first, gradient[6:], gradient[:6]), "core", SWAP)
    near, other = lax.optimization_barrier((spread_far(far), other))

    mine = exchange(near, NEAR)
    mine, other = lax.optimization_barrier((mine, other))
    theirs = lax.ppermute(mine, "core", SWAP)
    owned = in_order(first, keep[None], other[None], 0)
    new_params, new_moment, new_second = adam(owned, params, moment, second)
    gathered = write_bucket(theirs, True, write_bucket(mine, False))
    return (new_params, new_moment, new_second, gathered.reshape(2, D, COLS))


def solution(mesh):
    fine = Mesh(mesh.devices.reshape(SIZES), ALL)
    rows = P(None, ALL, None)
    return jax.shard_map(
        on_device,
        mesh=fine,
        in_specs=(P(ALL, None), rows, rows, rows, rows),
        out_specs=(rows, rows, rows, P()),
        check_vma=False,
    )
```
